32 devices in a mesh: dp: 8 (over z, x), tensor: 4 (over y, core).
Axes of the slice: x: 2, y: 2, z: 4, core: 2. Of those that a mesh axis runs over, the one named last changes fastest.
Arguments:
- tokens: bfloat16 [256, 6144], P('dp', 'tensor'), may hold values from -32 to 32
- gain_in: float32 [6144], P('tensor'), may hold values from 0.1 to 1.9
- shift_in: float32 [6144], P('tensor'), may hold values from -3 to 3
- up_weight: bfloat16 [6144, 24576], P('tensor', 'dp'), may hold values from -0.078125 to 0.078125
- up_bias: float32 [24576], P('dp'), may hold values from -3 to 3
- down_weight: bfloat16 [24576, 6144], P('dp', 'tensor'), may hold values from -1 to 1
- gain_out: float32 [6144], P('tensor'), may hold values from 0.1 to 1.9
- curvature: float32 [256, 6144], P('dp', 'tensor'), may hold values from 0.5 to 12
- up_tangent: bfloat16 [6144, 24576], P('tensor', 'dp'), may hold values from -0.078125 to 0.078125
- down_tangent: bfloat16 [24576, 6144], P('dp', 'tensor'), may hold values from -1 to 1
Outputs:
- up_product: float32 [6144, 24576], P('tensor', 'dp')
- down_product: float32 [24576, 6144], P('dp', 'tensor')
The draws below stay inside these ranges and needn't reach their ends.
All inputs are finite; a program needn't handle non-finite values.
Results may differ from the reference program's by a relative error of at most 0.003.
Values may be sent and summed in bfloat16 or wider, within the bound.
No kernel may reach another device: no remote copies, remote signals or barrier semaphores. Data moves between devices by JAX's collectives and lax.ppermute only.
A program may use at most 128 MiB of HBM per device.

```python
import math
import jax
import jax.numpy as jnp
from jax import lax

D = 6144
FF = 24576
TOKENS = 256


def shared_down(key):
    return jax.random.truncated_normal(key, -4.0, 4.0, (FF, D), jnp.float32)


def draw_tokens(key, part):
    key = jax.random.fold_in(key, 11)
    key_scale, key_base, key_rows = jax.random.split(key, 3)
    columns = jnp.arange(D, dtype=jnp.float32) / D
    column_scale = jnp.power(2.0, columns) * jnp.exp(jax.random.uniform(key_scale, (D,), jnp.float32, 0.0, 0.6931))
    base = jax.random.truncated_normal(key_base, -4.0, 4.0, (TOKENS, D), jnp.float32)
    row_scale = jnp.power(2.0, jax.random.uniform(key_rows, (TOKENS, 1), jnp.float32, 0.0, 1.0))
    values = 0.25 * base * column_scale * row_scale
    return values.astype(jnp.bfloat16)


def draw_curvature(key, part):
    key = jax.random.fold_in(key, 23)
    rising = jnp.power(3.0, jnp.arange(D, dtype=jnp.float32) / D)
    base = jnp.exp(jax.random.uniform(key, (TOKENS, D), jnp.float32, -0.6931, 1.3862))
    return (base * rising).astype(jnp.float32)


def draw_down_weight(key, part):
    shared = shared_down(key)
    return (shared * (1.0 / math.sqrt(FF))).astype(jnp.bfloat16)


def draw_down_tangent(key, part):
    shared = shared_down(key)
    key = jax.random.fold_in(key, 37)
    fresh = jax.random.truncated_normal(key, -4.0, 4.0, (FF, D), jnp.float32)
    values = 0.8 * shared + 0.6 * fresh
    return (values * (1.0 / math.sqrt(FF))).astype(jnp.bfloat16)


def level_of(own_key, dims, pieces, least, high):
    loudness, own = 1.0, jax.random.fold_in(own_key, 6)
    for axis_at, blocks in pieces:
        heights = jnp.exp(jax.random.uniform(jax.random.fold_in(own, axis_at), (blocks,), jnp.float32, least / len(pieces), high / len(pieces)))
        loudness = loudness * jnp.repeat(heights, dims[axis_at] // blocks).reshape([-1 if axis == axis_at else 1 for axis in range(len(dims))])
    return loudness


def scatter_about(own_key, dims, deviation, bound, cuts=(), held_as=jnp.bfloat16):
    factor_of = level_of(own_key, dims, cuts, -0.22, 0.18) if cuts else 1.0
    drawn = jax.random.normal(own_key, dims, jnp.float32) * deviation * factor_of
    return jnp.minimum(jnp.maximum(drawn, -bound), bound).astype(held_as)


def setup_inputs(seed: int = 0) -> dict:
    streams_of = jax.random.split(jax.random.key(seed), 11)
    tokens = draw_tokens(jax.random.fold_in(streams_of[10], 71), 0)
    gain_in = jnp.clip(1.0 + 0.18 * jax.random.normal(streams_of[1], (D,), jnp.float32), 0.1, 1.9)
    shift_in = scatter_about(streams_of[2], (D,), 0.5, 3.0, ((0, 4),), jnp.float32)
    up_weight = scatter_about(streams_of[3], (D, FF), D ** -0.5, 0.078125, ((0, 4), (1, 8)))
    up_bias = scatter_about(streams_of[4], (FF,), 0.5, 3.0, ((0, 8),), jnp.float32)
    down_weight = draw_down_weight(jax.random.fold_in(streams_of[10], 71), 0)
    gain_out = jnp.clip(1.0 + 0.18 * jax.random.normal(streams_of[6], (D,), jnp.float32), 0.1, 1.9)
    curvature = draw_curvature(jax.random.fold_in(streams_of[10], 71), 0)
    up_tangent = scatter_about(streams_of[8], (D, FF), D ** -0.5, 0.078125, ((0, 4), (1, 8)))
    down_tangent = draw_down_tangent(jax.random.fold_in(streams_of[10], 71), 0)
    return dict(tokens=tokens, gain_in=gain_in, shift_in=shift_in, up_weight=up_weight, up_bias=up_bias, down_weight=down_weight, gain_out=gain_out, curvature=curvature, up_tangent=up_tangent, down_tangent=down_tangent)


epsilon = 1e-05
root_half = 0.7071067811865476
inv_root_two_pi = 0.3989422804014327

def gelu_value(values):
    return 0.5 * values * (1.0 + lax.erf(values * root_half))

def gelu_slope(values):
    return 0.5 * (1.0 + lax.erf(values * root_half)) + values * jnp.exp(-0.5 * values * values) * inv_root_two_pi

def reference(tokens, gain_in, shift_in, up_weight, up_bias, down_weight, gain_out, curvature, up_tangent, down_tangent):
    source = tokens.astype(jnp.float32)
    center_in = lax.optimization_barrier(jnp.mean(source, axis=1, keepdims=True))
    spread_in = lax.optimization_barrier(jnp.mean(jnp.square(source - center_in), axis=1, keepdims=True))
    normed = ((source - center_in) * lax.rsqrt(spread_in + epsilon) * gain_in + shift_in).astype(jnp.bfloat16)
    pre_full = jnp.dot(normed, up_weight, preferred_element_type=jnp.float32) + up_bias
    tangent_pre = jnp.dot(normed, up_tangent, preferred_element_type=jnp.float32)
    hidden = gelu_value(pre_full).astype(jnp.bfloat16)
    slope_full = gelu_slope(pre_full)
    hidden_tangent = (slope_full * tangent_pre).astype(jnp.bfloat16)
    slope_kept = lax.optimization_barrier(slope_full.astype(jnp.bfloat16))
    output = source + jnp.dot(hidden, down_weight, preferred_element_type=jnp.float32)
    output_tangent = jnp.dot(hidden_tangent, down_weight, preferred_element_type=jnp.float32) + jnp.dot(hidden, down_tangent, preferred_element_type=jnp.float32)
    center_out = lax.optimization_barrier(jnp.mean(output, axis=1, keepdims=True))
    spread_out = lax.optimization_barrier(jnp.mean(jnp.square(output - center_out), axis=1, keepdims=True))
    inverse_out = lax.rsqrt(spread_out + epsilon)
    normal_out = (output - center_out) * inverse_out
    normal_tangent = (output_tangent - lax.optimization_barrier(jnp.mean(output_tangent, axis=1, keepdims=True)) - normal_out * lax.optimization_barrier(jnp.mean(normal_out * output_tangent, axis=1, keepdims=True))) * inverse_out
    weighted = gain_out * gain_out * curvature * normal_tangent
    cotangent = ((weighted - lax.optimization_barrier(jnp.mean(weighted, axis=1, keepdims=True)) - normal_out * lax.optimization_barrier(jnp.mean(normal_out * weighted, axis=1, keepdims=True))) * inverse_out).astype(jnp.bfloat16)
    down_product = jnp.dot(hidden.T, cotangent, preferred_element_type=jnp.float32)
    back_hidden = jnp.dot(cotangent, down_weight.T, preferred_element_type=jnp.float32)
    grad_pre = (back_hidden * slope_kept.astype(jnp.float32)).astype(jnp.bfloat16)
    up_product = jnp.dot(normed.T, grad_pre, preferred_element_type=jnp.float32)
    return (up_product, down_product)
```

```python
import functools

import jax
import jax.numpy as jnp
from jax import lax
from jax.experimental import pallas as pl
from jax.experimental.pallas import tpu as pltpu
from jax.sharding import PartitionSpec as P

D = 6144
TILE = 256
LANES = 128
LOADS = 4
SLOTS = 6
SCALE = 1000
BF16 = jnp.bfloat16
F32 = jnp.float32
PARAMS = pltpu.CompilerParams(vmem_limit_bytes=20 * 1024 * 1024)


epsilon = 1e-05
root_half = 0.7071067811865476
inv_root_two_pi = 0.3989422804014327


def swap_tensor(value, flip):
    size = lax.axis_size("tensor")
    return lax.ppermute(value, "tensor", [(t, t ^ flip) for t in range(size)])


def swap_dp(value, flip):
    size = lax.axis_size("dp")
    return lax.ppermute(value, "dp", [(i, i ^ flip) for i in range(size)])


def after(value, *earlier):
    return lax.optimization_barrier((value, *earlier))[0]


def swap_rows(values):
    half = values.shape[0] // 2
    return jnp.concatenate([values[half:], values[:half]], axis=0)


def far_bits():
    return [1 << k for k in range(1, lax.axis_size("dp").bit_length() - 1)]


def gather_rows(value, beside=None):
    half = value.shape[0] // 2
    count = lax.axis_size("dp")
    held = {0: value}
    for bit in reversed(far_bits()):
        held |= {far | bit: swap_dp(block, bit) for far, block in held.items()}
    held |= {far | 1: swap_dp(block, 1) for far, block in held.items()}
    made = beside(held[count - 2]) if beside else ()
    blocks = [held[place] for place in range(count - 1)] + [after(held[count - 1], *made)]
    rows = jnp.concatenate(
        [block[:half] for block in blocks] + [block[half:] for block in blocks], axis=0
    )
    return rows, made


def scatter_rows(parts, rows):
    half = rows // 2
    count = lax.axis_size("dp")

    def block(place):
        cuts = [
            part[k * count * half + place * half : k * count * half + (place + 1) * half]
            for part in parts
            for k in (0, 1)
        ]
        return jnp.concatenate(cuts, axis=0)

    order = list(range(count - 2, -1, -2))
    terms = {}
    for k, far in enumerate(order):
        sent = block(far + 1).astype(BF16)
        if k >= 1:
            sent = after(sent, *[terms[o][1] for o in order[: max(1, k - 1)]])
        terms[far] = [block(far), swap_dp(sent, 1)]
    pending = [(far, bit) for bit in far_bits() for far in order if far & bit and far & (bit - 1) < 2]
    pending.sort(key=lambda step: [-step[0], step[1]])
    last = []
    for far, bit in pending:
        total = sum(term.astype(F32) for term in terms[far]).astype(BF16)
        total = after(total, *last) if last else total
        last = [total]
        terms[far ^ bit].append(swap_dp(total, bit))
    return terms[0]


def whole(array):
    return pl.BlockSpec(array.shape, lambda *_: (0,) * array.ndim)


def cost(flops, *arrays):
    moved = sum(a.size * a.dtype.itemsize for a in arrays)
    return pl.CostEstimate(
        flops=int(flops) // SCALE, bytes_accessed=int(moved) // SCALE, transcendentals=0
    )


def load_kernel(start, count, *refs):
    refs, sems = refs[:count] + refs[-1 - count : -1], refs[-1]
    copies = []
    for k in range(count):
        given, held = refs[k], refs[count + k]
        rows, width = held.shape
        step = rows // LOADS
        for n in range(LOADS):
            cut = pl.ds(n * step, step)
            place = given.at[cut, pl.ds(start, width)]
            copies.append(pltpu.make_async_copy(place, held.at[cut], sems.at[k * LOADS + n]))
            copies[-1].start()
    for copy in copies:
        copy.wait()


def load_columns(arrays, start, width, *earlier):
    rows = arrays[0].shape[0]
    parts = [jax.ShapeDtypeStruct((rows, width), a.dtype) for a in arrays]
    return pl.pallas_call(
        functools.partial(load_kernel, start, len(arrays)),
        in_specs=[pl.BlockSpec(memory_space=pl.ANY)] * (len(arrays) + len(earlier)),
        out_specs=[pl.BlockSpec(memory_space=pltpu.VMEM)] * len(arrays),
        out_shape=[pltpu.VMEM(p.shape, p.dtype) for p in parts],
        scratch_shapes=[pltpu.SemaphoreType.DMA((LOADS * len(arrays),))],
        compiler_params=PARAMS,
        cost_estimate=cost(0, *parts),
        name="load_columns",
    )(*[pltpu.with_memory_space_constraint(a, pltpu.HBM) for a in arrays], *earlier)


def up_kernel(rows_ref, weight_ref, tangent_ref, own_ref, other_ref):
    half = own_ref.shape[1]
    for start in range(0, own_ref.shape[2], TILE):
        cut = slice(start, start + TILE)
        for k, ref in enumerate((weight_ref, tangent_ref)):
            part = jnp.dot(rows_ref[...], ref[:, cut], preferred_element_type=F32)
            own_ref[k, :, cut] = part[:half]
            other_ref[k, :, cut] = part[half:].astype(BF16)


def up_parts(normed, weight, tangent):
    rows, width = normed.shape
    half, chunk = rows // 2, weight.shape[1]
    out_shape = (
        jax.ShapeDtypeStruct((2, half, chunk), F32),
        jax.ShapeDtypeStruct((2, half, chunk), BF16),
    )
    held = [pltpu.with_memory_space_constraint(a, pltpu.VMEM) for a in (weight, tangent)]
    return pl.pallas_call(
        up_kernel,
        out_shape=out_shape,
        compiler_params=PARAMS,
        cost_estimate=cost(4 * rows * width * chunk, normed),
        name="up_parts",
    )(normed, *held)


def back_kernel(rows_ref, weight_ref, *refs):
    own_ref, other_ref = refs[-2:]
    half = own_ref.shape[0]
    part = lax.dot_general(
        rows_ref[...], weight_ref[...], (((1,), (1,)), ((), ())), preferred_element_type=F32
    )
    own_ref[...] = part[:half]
    other_ref[...] = part[half:].astype(BF16)


def back_parts(cotangent, weight, start, chunk, *earlier):
    rows, width = cotangent.shape
    half = rows // 2
    first = start // TILE
    out_spec = pl.BlockSpec((half, TILE), lambda i: (0, i))
    out_shape = (
        jax.ShapeDtypeStruct((half, chunk), F32),
        jax.ShapeDtypeStruct((half, chunk), BF16),
    )
    moved = jax.ShapeDtypeStruct((width, chunk), BF16)
    return pl.pallas_call(
        back_kernel,
        grid=(chunk // TILE,),
        in_specs=[whole(cotangent), pl.BlockSpec((TILE, width), lambda i: (first + i, 0))]
        + [pl.BlockSpec(memory_space=pl.ANY)] * len(earlier),
        out_specs=(out_spec, out_spec),
        out_shape=out_shape,
        compiler_params=PARAMS,
        cost_estimate=cost(2 * rows * width * chunk, cotangent, moved),
        name="back_parts",
    )(cotangent, weight, *earlier)


def outer(left, right):
    return lax.dot_general(left, right, (((0,), (0,)), ((), ())), preferred_element_type=F32)


def columns_kernel(column, left_ref, right_ref, *refs):
    out_ref, held, sems = refs[-3:]
    width = right_ref.shape[1]
    copies = []
    for k in range(held.shape[0]):
        held[k] = outer(left_ref[:, k * TILE : (k + 1) * TILE], right_ref[...])
        place = out_ref.at[pl.ds(k * TILE, TILE), pl.ds(column, width)]
        copies.append(pltpu.make_async_copy(held.at[k], place, sems.at[k]))
        copies[-1].start()
    for copy in copies:
        copy.wait()


def outer_columns(left, right, shape, column, so_far):
    tiles = left.shape[1] // TILE
    moved = jax.ShapeDtypeStruct((left.shape[1], right.shape[1]), F32)
    vmem, anywhere = pl.BlockSpec(memory_space=pltpu.VMEM), pl.BlockSpec(memory_space=pl.ANY)
    more = [] if so_far is None else [so_far]
    return pl.pallas_call(
        functools.partial(columns_kernel, column),
        in_specs=[vmem, vmem] + [anywhere] * len(more),
        out_specs=anywhere,
        out_shape=jax.ShapeDtypeStruct(shape, F32),
        scratch_shapes=[
            pltpu.VMEM((tiles, TILE, right.shape[1]), F32),
            pltpu.SemaphoreType.DMA((tiles,)),
        ],
        input_output_aliases={2: 0} if more else {},
        compiler_params=PARAMS,
        cost_estimate=cost(2 * left.size * right.shape[1], left, right, moved),
        name="outer_columns",
    )(left, right, *more)


def rows_kernel(count, *refs):
    left_refs, right_ref = refs[:count], refs[count]
    out_ref, held, sems = refs[-3:]
    slots = held.shape[0]
    copies = []
    for left_ref in left_refs:
        for start in range(0, left_ref.shape[1], TILE):
            k = len(copies)
            slot = k % slots
            if k >= slots:
                copies[k - slots].wait()
            held[slot] = outer(left_ref[:, start : start + TILE], right_ref[...])
            place = out_ref.at[pl.ds(k * TILE, TILE)]
            copies.append(pltpu.make_async_copy(held.at[slot], place, sems.at[slot]))
            copies[k].start()
    for copy in copies[-slots:]:
        copy.wait()


def outer_rows(lefts, right, shape, *earlier):
    slots = min(SLOTS, shape[0] // TILE)
    vmem = pl.BlockSpec(memory_space=pltpu.VMEM)
    moved = jax.ShapeDtypeStruct(shape, F32)
    return pl.pallas_call(
        functools.partial(rows_kernel, len(lefts)),
        in_specs=[vmem] * (len(lefts) + 1) + [pl.BlockSpec(memory_space=pl.ANY)] * len(earlier),
        out_specs=pl.BlockSpec(memory_space=pl.ANY),
        out_shape=moved,
        scratch_shapes=[
            pltpu.VMEM((slots, TILE, shape[1]), F32),
            pltpu.SemaphoreType.DMA((slots,)),
        ],
        compiler_params=PARAMS,
        cost_estimate=cost(2 * right.size * shape[0], right, moved),
        name="outer_rows",
    )(*lefts, right, *earlier)


def row_sum(values):
    return jnp.sum(values, axis=1, keepdims=True)


def put_columns(ref, values):
    lane = lax.broadcasted_iota(jnp.int32, ref.shape, 1)
    total = jnp.zeros(ref.shape, F32)
    for k, value in enumerate(values):
        total = jnp.where(lane == k, value, total)
    ref[...] = total


def get_columns(refs, count):
    found = []
    for flip, ref in enumerate(refs):
        values = ref[...]
        if flip & 1:
            values = swap_rows(values)
        found.append([values[:, k : k + 1] for k in range(count)])
    return found


def swap_if(flag, values):
    return jnp.where(flag == 1, swap_rows(values), values)


def stats_in_kernel(odd_ref, given_ref, tokens_ref, stats_ref):
    tokens_ref[...] = swap_if(odd_ref[0], given_ref[...])
    source = tokens_ref[...].astype(F32)
    mean = row_sum(source) / source.shape[1]
    put_columns(stats_ref, [mean, row_sum(jnp.square(source - mean))])


def norm_in_kernel(tokens_ref, gain_ref, shift_ref, *refs):
    source = tokens_ref[...].astype(F32)
    width = source.shape[1]
    stats = get_columns(refs[:-1], 2)
    center = sum(s[0] for s in stats) / len(stats)
    spread = sum(s[1] + width * jnp.square(s[0] - center) for s in stats) / D
    inverse = lax.rsqrt(spread + epsilon)
    refs[-1][...] = ((source - center) * inverse * gain_ref[...] + shift_ref[...]).astype(BF16)


def stats_out_kernel(tokens_ref, gain_ref, curvature_ref, *refs):
    *terms, output_ref, tangent_ref, stats_ref = refs
    rows, width = output_ref.shape
    total = sum(term[...].astype(F32) for term in terms)
    output = tokens_ref[...].astype(F32) + total[:rows]
    tangent = total[rows:]
    output_ref[...] = output
    tangent_ref[...] = tangent
    factor = gain_ref[...] * gain_ref[...] * curvature_ref[...]
    output_mean, tangent_mean = row_sum(output) / width, row_sum(tangent) / width
    output_off, tangent_off = output - output_mean, tangent - tangent_mean
    factor_output = factor * output_off
    put_columns(
        stats_ref,
        [
            output_mean,
            tangent_mean,
            row_sum(output_off * output_off),
            row_sum(output_off * tangent_off),
            row_sum(factor),
            row_sum(factor_output),
            row_sum(factor * tangent_off),
            row_sum(factor_output * output_off),
            row_sum(factor_output * tangent_off),
        ],
    )


def cotangent_kernel(output_ref, tangent_ref, gain_ref, curvature_ref, *refs):
    output, tangent = output_ref[...], tangent_ref[...]
    width = output.shape[1]
    stats = get_columns(refs[:-1], 9)
    center = sum(s[0] for s in stats) / len(stats)
    center_tangent = sum(s[1] for s in stats) / len(stats)
    square = cross = f_output = f_tangent = f_square = f_cross = 0.0
    for mean_o, mean_t, oo, ot, f, fo, ft, foo, fot in stats:
        a, b = mean_o - center, mean_t - center_tangent
        square += oo + width * a * a
        cross += ot + width * a * b
        f_output += fo + a * f
        f_tangent += ft + b * f
        f_square += foo + a * (2.0 * fo + a * f)
        f_cross += fot + a * ft + b * (fo + a * f)
    inverse = lax.rsqrt(square / D + epsilon)
    tangent_dot = cross * inverse / D
    weight_mean = (f_tangent - tangent_dot * inverse * f_output) * inverse / D
    weight_dot = (f_cross - tangent_dot * inverse * f_square) * inverse * inverse / D
    normal = (output - center) * inverse
    factor = gain_ref[...] * gain_ref[...] * curvature_ref[...]
    weighted = factor * ((tangent - center_tangent - normal * tangent_dot) * inverse)
    refs[-1][...] = ((weighted - weight_mean - normal * weight_dot) * inverse).astype(BF16)


def in_vmem(kernel, out_shape, *operands):
    return pl.pallas_call(
        kernel,
        out_shape=out_shape,
        compiler_params=PARAMS,
        cost_estimate=cost(0, *operands),
        name=kernel.__name__,
    )(*operands)


def peers(value):
    return [value] + [swap_tensor(value, flip) for flip in range(1, lax.axis_size("tensor"))]


def over_tensor(total, *earlier):
    flip = 2
    while flip < lax.axis_size("tensor"):
        received = swap_tensor(total.astype(BF16), flip)
        if earlier:
            received = after(received, *earlier)
        total = total + received.astype(F32)
        flip *= 2
    return total


def chunks_of(units):
    part = units // 6
    sizes = [part, 2 * part, 2 * part, part] if part % TILE == 0 else [units]
    return [sum(sizes[:k]) for k in range(len(sizes))], sizes


def on_device(
    tokens,
    gain_in,
    shift_in,
    up_weight,
    up_bias,
    down_weight,
    gain_out,
    curvature,
    up_tangent,
    down_tangent,
):
    rows, width = tokens.shape
    hidden_units = up_weight.shape[1]
    starts, sizes = chunks_of(hidden_units)
    odd = lax.axis_index("tensor") & 1
    curvature = swap_if(odd, curvature)
    gain_in, shift_in, gain_out = gain_in[None], shift_in[None], gain_out[None]
    stats_shape = jax.ShapeDtypeStruct((rows, LANES), F32)
    rows_bf16 = jax.ShapeDtypeStruct((rows, width), BF16)
    rows_f32 = jax.ShapeDtypeStruct((rows, width), F32)

    tokens, stats = pl.pallas_call(
        stats_in_kernel,
        in_specs=[
            pl.BlockSpec(memory_space=pltpu.SMEM),
            pl.BlockSpec(memory_space=pltpu.VMEM),
        ],
        out_shape=(rows_bf16, stats_shape),
        compiler_params=PARAMS,
        cost_estimate=cost(0, tokens),
        name="stats_in_kernel",
    )(odd.astype(jnp.int32)[None], tokens)
    stats = peers(stats)
    normed = in_vmem(norm_in_kernel, rows_bf16, tokens, gain_in, shift_in, *stats)
    all_normed, weights = gather_rows(
        normed,
        lambda early: load_columns((after(up_weight, early), up_tangent), starts[0], sizes[0]),
    )

    totals, owns, own = [], [], None
    for j, (start, chunk) in enumerate(zip(starts, sizes)):
        if j:
            weights = load_columns((after(up_weight, own), up_tangent), start, chunk, totals[-1])
        lhs = after(all_normed, totals[-1], *weights) if j else all_normed
        own, other = up_parts(lhs, *weights)
        totals.append(own + swap_tensor(other, 1).astype(F32))
        owns.append(own)

    slopes, hiddens, done = [], [], [()]
    primal = tangent = None
    for j, (start, chunk) in enumerate(zip(starts, sizes)):
        total = over_tensor(totals[j], *([both if j == len(starts) - 1 else mine, *done[j - 1]] if j else owns[1:2]))
        if j:
            total = after(total, totals[min(j + 2, len(totals) - 1)])
        pre = total[0] + up_bias[start : start + chunk]
        cumulative = 0.5 * (1.0 + lax.erf(pre * root_half))
        slope = cumulative + pre * jnp.exp(-0.5 * pre * pre) * inv_root_two_pi
        slopes.append(slope.astype(BF16))
        mine = jnp.stack([(pre * cumulative).astype(BF16), (slope * total[1]).astype(BF16)])
        both = jnp.concatenate([mine, swap_tensor(mine, 1)], axis=1)
        hidden, hidden_tangent = both[0], both[1]
        hiddens.append(hidden)
        weight = down_weight[start : start + chunk]
        primal_part = jnp.dot(hidden, weight, preferred_element_type=F32)
        tangent_part = jnp.dot(hidden_tangent, weight, preferred_element_type=F32) + jnp.dot(
            hidden, down_tangent[start : start + chunk], preferred_element_type=F32
        )
        primal = primal_part if primal is None else primal + primal_part
        tangent = tangent_part if tangent is None else tangent + tangent_part
        done.append((primal, tangent))

    terms = scatter_rows([primal, tangent], rows)
    output, output_tangent, stats = in_vmem(
        stats_out_kernel,
        (rows_f32, rows_f32, stats_shape),
        tokens,
        gain_out,
        curvature,
        *terms,
    )
    cotangent = in_vmem(
        cotangent_kernel,
        rows_bf16,
        output,
        output_tangent,
        gain_out,
        curvature,
        *peers(stats),
    )
    all_cotangent, _ = gather_rows(cotangent)

    merged = 2 if len(starts) > 2 else 1
    slopes = [jnp.concatenate(slopes[:merged], axis=1)] + slopes[merged:]
    sizes = [sum(sizes[:merged])] + sizes[merged:]
    starts = [0] + starts[merged:]
    totals, lhs = [], all_cotangent
    for start, chunk in zip(starts, sizes):
        own, other = back_parts(lhs, down_weight, start, chunk, *totals[:-1])
        totals.append(own + swap_tensor(other, 1).astype(F32))
        lhs = after(all_cotangent, own)
    down_product = outer_rows(hiddens, all_cotangent, down_weight.shape, *totals)

    made = [down_product]
    for j, (start, chunk) in enumerate(zip(starts, sizes)):
        total = over_tensor(totals[j], made[max(0, j - 1)])
        grad = (total * slopes[j].astype(F32)).astype(BF16)
        grad = jnp.concatenate([grad, swap_tensor(grad, 1)], axis=0)
        so_far = made[-1] if j else None
        made.append(outer_columns(all_normed, grad, up_weight.shape, start, so_far))
    up_product = made[-1]
    return (up_product, down_product)


def solution(mesh):
    return jax.shard_map(
        on_device,
        mesh=mesh,
        in_specs=(
            P("dp", "tensor"),
            P("tensor"),
            P("tensor"),
            P("tensor", "dp"),
            P("dp"),
            P("dp", "tensor"),
            P("tensor"),
            P("dp", "tensor"),
            P("tensor", "dp"),
            P("dp", "tensor"),
        ),
        out_specs=(P("tensor", "dp"), P("dp", "tensor")),
        check_vma=False,
    )
```

```python
import functools

import jax
import jax.numpy as jnp
from jax import lax
from jax.experimental import pallas as pl
from jax.experimental.pallas import tpu as pltpu
from jax.sharding import PartitionSpec as P

D = 6144
TILE = 256
LANES = 128
LOADS = 4
SLOTS = 6
SCALE = 1000
BF16 = jnp.bfloat16
F32 = jnp.float32
PARAMS = pltpu.CompilerParams(vmem_limit_bytes=20 * 1024 * 1024)


epsilon = 1e-05
root_half = 0.7071067811865476
inv_root_two_pi = 0.3989422804014327


def swap_tensor(value, flip):
    size = lax.axis_size("tensor")
    return lax.ppermute(value, "tensor", [(t, t ^ flip) for t in range(size)])


def swap_dp(value, flip):
    size = lax.axis_size("dp")
    return lax.ppermute(value, "dp", [(i, i ^ flip) for i in range(size)])


def after(value, *earlier):
    return lax.optimization_barrier((value, *earlier))[0]


def swap_rows(values):
    half = values.shape[0] // 2
    return jnp.concatenate([values[half:], values[:half]], axis=0)


def far_bits():
    return [1 << k for k in range(1, lax.axis_size("dp").bit_length() - 1)]


def gather_rows(value, beside=None):
    half = value.shape[0] // 2
    count = lax.axis_size("dp")
    held = {0: value}
    for bit in reversed(far_bits()):
        held |= {far | bit: swap_dp(block, bit) for far, block in held.items()}
    held |= {far | 1: swap_dp(block, 1) for far, block in held.items()}
    made = beside(held[count - 2]) if beside else ()
    blocks = [held[place] for place in range(count - 1)] + [after(held[count - 1], *made)]
    rows = jnp.concatenate(
        [block[:half] for block in blocks] + [block[half:] for block in blocks], axis=0
    )
    return rows, made


def scatter_rows(parts, rows):
    half = rows // 2
    count = lax.axis_size("dp")

    def block(place):
        cuts = [
            part[k * count * half + place * half : k * count * half + (place + 1) * half]
            for part in parts
            for k in (0, 1)
        ]
        return jnp.concatenate(cuts, axis=0)

    order = list(range(count - 2, -1, -2))
    terms = {}
    for k, far in enumerate(order):
        sent = block(far + 1).astype(BF16)
        if k >= 2:
            sent = after(sent, *[terms[o][1] for o in order[: k - 1]])
        terms[far] = [block(far), swap_dp(sent, 1)]
    pending = [(far, bit) for bit in far_bits() for far in order if far & bit and far & (bit - 1) < 2]
    pending.sort(key=lambda step: [-step[0], step[1]])
    last = []
    for far, bit in pending:
        total = sum(term.astype(F32) for term in terms[far]).astype(BF16)
        total = after(total, *last) if last else total
        last = [total]
        terms[far ^ bit].append(swap_dp(total, bit))
    return terms[0], last[0]


def cost(flops, *arrays):
    moved = sum(a.size * a.dtype.itemsize for a in arrays)
    return pl.CostEstimate(
        flops=int(flops) // SCALE, bytes_accessed=int(moved) // SCALE, transcendentals=0
    )


def load_kernel(start, count, *refs):
    refs, sems = refs[:count] + refs[-1 - count : -1], refs[-1]
    copies = []
    for k in range(count):
        given, held = refs[k], refs[count + k]
        rows, width = held.shape
        step = rows // LOADS
        for n in range(LOADS):
            cut = pl.ds(n * step, step)
            place = given.at[cut, pl.ds(start, width)]
            copies.append(pltpu.make_async_copy(place, held.at[cut], sems.at[k * LOADS + n]))
            copies[-1].start()
    for copy in copies:
        copy.wait()


def load_columns(arrays, start, width, *earlier):
    rows = arrays[0].shape[0]
    parts = [jax.ShapeDtypeStruct((rows, width), a.dtype) for a in arrays]
    return pl.pallas_call(
        functools.partial(load_kernel, start, len(arrays)),
        in_specs=[pl.BlockSpec(memory_space=pl.ANY)] * (len(arrays) + len(earlier)),
        out_specs=[pl.BlockSpec(memory_space=pltpu.VMEM)] * len(arrays),
        out_shape=[pltpu.VMEM(p.shape, p.dtype) for p in parts],
        scratch_shapes=[pltpu.SemaphoreType.DMA((LOADS * len(arrays),))],
        compiler_params=PARAMS,
        cost_estimate=cost(0, *parts),
        name="load_columns",
    )(*[pltpu.with_memory_space_constraint(a, pltpu.HBM) for a in arrays], *earlier)


def load_rows(array, start, height, *earlier):
    def kernel(given_ref, *refs):
        held, sems = refs[-2:]
        step = height // LOADS
        copies = []
        for n in range(LOADS):
            place = given_ref.at[pl.ds(start + n * step, step)]
            copies.append(pltpu.make_async_copy(place, held.at[pl.ds(n * step, step)], sems.at[n]))
            copies[n].start()
        for copy in copies:
            copy.wait()

    return pl.pallas_call(
        kernel,
        in_specs=[pl.BlockSpec(memory_space=pl.ANY)] * (1 + len(earlier)),
        out_specs=pl.BlockSpec(memory_space=pltpu.VMEM),
        out_shape=pltpu.VMEM((height, array.shape[1]), array.dtype),
        scratch_shapes=[pltpu.SemaphoreType.DMA((LOADS,))],
        compiler_params=PARAMS,
        cost_estimate=cost(0, array),
        name="load_rows",
    )(pltpu.with_memory_space_constraint(array, pltpu.HBM), *earlier)


def back_kernel(first, rows_ref, weight_ref, *refs):
    own_ref, other_ref = refs[-2:]
    half, chunk = own_ref.shape
    for start in range(0, chunk, TILE):
        part = lax.dot_general(
            rows_ref[...],
            weight_ref[first + start : first + start + TILE],
            (((1,), (1,)), ((), ())),
            preferred_element_type=F32,
        )
        own_ref[:, start : start + TILE] = part[:half]
        other_ref[:, start : start + TILE] = part[half:].astype(BF16)


def back_parts(cotangent, weight, start, chunk, *earlier):
    rows, width = cotangent.shape
    half = rows // 2
    vmem, anywhere = pl.BlockSpec(memory_space=pltpu.VMEM), pl.BlockSpec(memory_space=pl.ANY)
    return pl.pallas_call(
        functools.partial(back_kernel, start),
        in_specs=[vmem, vmem] + [anywhere] * len(earlier),
        out_shape=(
            jax.ShapeDtypeStruct((half, chunk), F32),
            jax.ShapeDtypeStruct((half, chunk), BF16),
        ),
        compiler_params=PARAMS,
        cost_estimate=cost(2 * rows * width * chunk, cotangent),
        name="back_parts",
    )(cotangent, pltpu.with_memory_space_constraint(weight, pltpu.VMEM), *earlier)


def up_kernel(rows_ref, weight_ref, tangent_ref, own_ref, other_ref):
    half = own_ref.shape[1]
    for start in range(0, own_ref.shape[2], TILE):
        cut = slice(start, start + TILE)
        for k, ref in enumerate((weight_ref, tangent_ref)):
            part = jnp.dot(rows_ref[...], ref[:, cut], preferred_element_type=F32)
            own_ref[k, :, cut] = part[:half]
            other_ref[k, :, cut] = part[half:].astype(BF16)


def up_parts(normed, weight, tangent):
    rows, width = normed.shape
    half, chunk = rows // 2, weight.shape[1]
    out_shape = (
        jax.ShapeDtypeStruct((2, half, chunk), F32),
        jax.ShapeDtypeStruct((2, half, chunk), BF16),
    )
    held = [pltpu.with_memory_space_constraint(a, pltpu.VMEM) for a in (weight, tangent)]
    return pl.pallas_call(
        up_kernel,
        out_shape=out_shape,
        compiler_params=PARAMS,
        cost_estimate=cost(4 * rows * width * chunk, normed),
        name="up_parts",
    )(normed, *held)


def outer(left, right):
    return lax.dot_general(left, right, (((0,), (0,)), ((), ())), preferred_element_type=F32)


def columns_kernel(column, left_ref, right_ref, *refs):
    out_ref, held, sems = refs[-3:]
    width = right_ref.shape[1]
    copies = []
    for k in range(held.shape[0]):
        held[k] = outer(left_ref[:, k * TILE : (k + 1) * TILE], right_ref[...])
        place = out_ref.at[pl.ds(k * TILE, TILE), pl.ds(column, width)]
        copies.append(pltpu.make_async_copy(held.at[k], place, sems.at[k]))
        copies[-1].start()
    for copy in copies:
        copy.wait()


def outer_columns(left, right, shape, column, so_far):
    tiles = left.shape[1] // TILE
    moved = jax.ShapeDtypeStruct((left.shape[1], right.shape[1]), F32)
    vmem, anywhere = pl.BlockSpec(memory_space=pltpu.VMEM), pl.BlockSpec(memory_space=pl.ANY)
    more = [] if so_far is None else [so_far]
    return pl.pallas_call(
        functools.partial(columns_kernel, column),
        in_specs=[vmem, vmem] + [anywhere] * len(more),
        out_specs=anywhere,
        out_shape=jax.ShapeDtypeStruct(shape, F32),
        scratch_shapes=[
            pltpu.VMEM((tiles, TILE, right.shape[1]), F32),
            pltpu.SemaphoreType.DMA((tiles,)),
        ],
        input_output_aliases={2: 0} if more else {},
        compiler_params=PARAMS,
        cost_estimate=cost(2 * left.size * right.shape[1], left, right, moved),
        name="outer_columns",
    )(left, right, *more)


def rows_kernel(count, *refs):
    left_refs, right_ref = refs[:count], refs[count]
    out_ref, held, sems = refs[-3:]
    slots = held.shape[0]
    copies = []
    for left_ref in left_refs:
        for start in range(0, left_ref.shape[1], TILE):
            k = len(copies)
            slot = k % slots
            if k >= slots:
                copies[k - slots].wait()
            held[slot] = outer(left_ref[:, start : start + TILE], right_ref[...])
            place = out_ref.at[pl.ds(k * TILE, TILE)]
            copies.append(pltpu.make_async_copy(held.at[slot], place, sems.at[slot]))
            copies[k].start()
    for copy in copies[-slots:]:
        copy.wait()


def outer_rows(lefts, right, shape, *earlier):
    slots = min(SLOTS, shape[0] // TILE)
    vmem = pl.BlockSpec(memory_space=pltpu.VMEM)
    moved = jax.ShapeDtypeStruct(shape, F32)
    return pl.pallas_call(
        functools.partial(rows_kernel, len(lefts)),
        in_specs=[vmem] * (len(lefts) + 1) + [pl.BlockSpec(memory_space=pl.ANY)] * len(earlier),
        out_specs=pl.BlockSpec(memory_space=pl.ANY),
        out_shape=moved,
        scratch_shapes=[
            pltpu.VMEM((slots, TILE, shape[1]), F32),
            pltpu.SemaphoreType.DMA((slots,)),
        ],
        compiler_params=PARAMS,
        cost_estimate=cost(2 * right.size * shape[0], right, moved),
        name="outer_rows",
    )(*lefts, right, *earlier)


def row_sum(values):
    return jnp.sum(values, axis=1, keepdims=True)


def put_columns(ref, values):
    lane = lax.broadcasted_iota(jnp.int32, ref.shape, 1)
    total = jnp.zeros(ref.shape, F32)
    for k, value in enumerate(values):
        total = jnp.where(lane == k, value, total)
    ref[...] = total


def get_columns(refs, count):
    found = []
    for flip, ref in enumerate(refs):
        values = ref[...]
        if flip & 1:
            values = swap_rows(values)
        found.append([values[:, k : k + 1] for k in range(count)])
    return found


def swap_if(flag, values):
    return jnp.where(flag == 1, swap_rows(values), values)


def stats_in_kernel(odd_ref, given_ref, tokens_ref, stats_ref):
    tokens_ref[...] = swap_if(odd_ref[0], given_ref[...])
    source = tokens_ref[...].astype(F32)
    mean = row_sum(source) / source.shape[1]
    put_columns(stats_ref, [mean, row_sum(jnp.square(source - mean))])


def norm_in_kernel(tokens_ref, gain_ref, shift_ref, *refs):
    source = tokens_ref[...].astype(F32)
    width = source.shape[1]
    stats = get_columns(refs[:-1], 2)
    center = sum(s[0] for s in stats) / len(stats)
    spread = sum(s[1] + width * jnp.square(s[0] - center) for s in stats) / D
    inverse = lax.rsqrt(spread + epsilon)
    refs[-1][...] = ((source - center) * inverse * gain_ref[...] + shift_ref[...]).astype(BF16)


def stats_out_kernel(count, tokens_ref, gain_ref, curvature_ref, *refs):
    terms = refs[:count]
    output_ref, tangent_ref, stats_ref = refs[-3:]
    rows, width = output_ref.shape
    total = sum(term[...].astype(F32) for term in terms)
    output = tokens_ref[...].astype(F32) + total[:rows]
    tangent = total[rows:]
    output_ref[...] = output
    tangent_ref[...] = tangent
    factor = gain_ref[...] * gain_ref[...] * curvature_ref[...]
    output_mean, tangent_mean = row_sum(output) / width, row_sum(tangent) / width
    output_off, tangent_off = output - output_mean, tangent - tangent_mean
    factor_output = factor * output_off
    put_columns(
        stats_ref,
        [
            output_mean,
            tangent_mean,
            row_sum(output_off * output_off),
            row_sum(output_off * tangent_off),
            row_sum(factor),
            row_sum(factor_output),
            row_sum(factor * tangent_off),
            row_sum(factor_output * output_off),
            row_sum(factor_output * tangent_off),
        ],
    )


def cotangent_kernel(output_ref, tangent_ref, gain_ref, curvature_ref, *refs):
    output, tangent = output_ref[...], tangent_ref[...]
    width = output.shape[1]
    stats = get_columns(refs[:-1], 9)
    center = sum(s[0] for s in stats) / len(stats)
    center_tangent = sum(s[1] for s in stats) / len(stats)
    square = cross = f_output = f_tangent = f_square = f_cross = 0.0
    for mean_o, mean_t, oo, ot, f, fo, ft, foo, fot in stats:
        a, b = mean_o - center, mean_t - center_tangent
        square += oo + width * a * a
        cross += ot + width * a * b
        f_output += fo + a * f
        f_tangent += ft + b * f
        f_square += foo + a * (2.0 * fo + a * f)
        f_cross += fot + a * ft + b * (fo + a * f)
    inverse = lax.rsqrt(square / D + epsilon)
    tangent_dot = cross * inverse / D
    weight_mean = (f_tangent - tangent_dot * inverse * f_output) * inverse / D
    weight_dot = (f_cross - tangent_dot * inverse * f_square) * inverse * inverse / D
    normal = (output - center) * inverse
    factor = gain_ref[...] * gain_ref[...] * curvature_ref[...]
    weighted = factor * ((tangent - center_tangent - normal * tangent_dot) * inverse)
    refs[-1][...] = ((weighted - weight_mean - normal * weight_dot) * inverse).astype(BF16)


def in_vmem(kernel, out_shape, *operands):
    return pl.pallas_call(
        kernel,
        out_shape=out_shape,
        compiler_params=PARAMS,
        cost_estimate=cost(0, *operands),
        name=kernel.__name__,
    )(*operands)


def peers(value):
    return [value] + [swap_tensor(value, flip) for flip in range(1, lax.axis_size("tensor"))]


def over_tensor(total, *earlier):
    flip = 2
    while flip < lax.axis_size("tensor"):
        received = swap_tensor(total.astype(BF16), flip)
        if earlier:
            received = after(received, *earlier)
        total = total + received.astype(F32)
        flip *= 2
    return total


def chunks_of(units):
    part = units // 6
    sizes = [part, 2 * part, 2 * part, part] if part % TILE == 0 else [units]
    return [sum(sizes[:k]) for k in range(len(sizes))], sizes


def on_device(
    tokens,
    gain_in,
    shift_in,
    up_weight,
    up_bias,
    down_weight,
    gain_out,
    curvature,
    up_tangent,
    down_tangent,
):
    rows, width = tokens.shape
    hidden_units = up_weight.shape[1]
    starts, sizes = chunks_of(hidden_units)
    odd = lax.axis_index("tensor") & 1
    curvature = swap_if(odd, curvature)
    gain_in, shift_in, gain_out = gain_in[None], shift_in[None], gain_out[None]
    stats_shape = jax.ShapeDtypeStruct((rows, LANES), F32)
    rows_bf16 = jax.ShapeDtypeStruct((rows, width), BF16)
    rows_f32 = jax.ShapeDtypeStruct((rows, width), F32)

    tokens, stats = pl.pallas_call(
        stats_in_kernel,
        in_specs=[
            pl.BlockSpec(memory_space=pltpu.SMEM),
            pl.BlockSpec(memory_space=pltpu.VMEM),
        ],
        out_shape=(rows_bf16, stats_shape),
        compiler_params=PARAMS,
        cost_estimate=cost(0, tokens),
        name="stats_in_kernel",
    )(odd.astype(jnp.int32)[None], tokens)
    stats = peers(stats)
    normed = in_vmem(norm_in_kernel, rows_bf16, tokens, gain_in, shift_in, *stats)
    all_normed, weights = gather_rows(
        normed,
        lambda early: load_columns((after(up_weight, early), up_tangent), starts[0], sizes[0]),
    )

    totals, owns, own = [], [], None
    for j, (start, chunk) in enumerate(zip(starts, sizes)):
        if j:
            weights = load_columns((after(up_weight, own), up_tangent), start, chunk, totals[-1])
        lhs = after(all_normed, totals[-1], *weights) if j else all_normed
        own, other = up_parts(lhs, *weights)
        totals.append(own + swap_tensor(other, 1).astype(F32))
        owns.append(own)

    slopes, hiddens, done = [], [], [()]
    primal = tangent = None
    for j, (start, chunk) in enumerate(zip(starts, sizes)):
        total = over_tensor(totals[j], *([both if j == len(starts) - 1 else mine, *done[j - 1]] if j else owns[1:2]))
        if j:
            total = after(total, totals[min(j + 2, len(totals) - 1)])
        pre = total[0] + up_bias[start : start + chunk]
        cumulative = 0.5 * (1.0 + lax.erf(pre * root_half))
        slope = cumulative + pre * jnp.exp(-0.5 * pre * pre) * inv_root_two_pi
        slopes.append(slope.astype(BF16))
        mine = jnp.stack([(pre * cumulative).astype(BF16), (slope * total[1]).astype(BF16)])
        both = jnp.concatenate([mine, swap_tensor(mine, 1)], axis=1)
        hidden, hidden_tangent = both[0], both[1]
        hiddens.append(hidden)
        weight = down_weight[start : start + chunk]
        primal_part = jnp.dot(hidden, weight, preferred_element_type=F32)
        tangent_part = jnp.dot(hidden_tangent, weight, preferred_element_type=F32) + jnp.dot(
            hidden, down_tangent[start : start + chunk], preferred_element_type=F32
        )
        primal = primal_part if primal is None else primal + primal_part
        tangent = tangent_part if tangent is None else tangent + tangent_part
        done.append((primal, tangent))

    terms, step = scatter_rows([primal, tangent], rows)
    held = load_rows(down_weight, 0, hidden_units, step)
    operands = [tokens, gain_out, curvature, *terms]
    vmem = pl.BlockSpec(memory_space=pltpu.VMEM)
    output, output_tangent, stats = pl.pallas_call(
        functools.partial(stats_out_kernel, len(terms)),
        in_specs=[vmem] * len(operands) + [pl.BlockSpec(memory_space=pl.ANY)],
        out_shape=(rows_f32, rows_f32, stats_shape),
        compiler_params=PARAMS,
        cost_estimate=cost(0, *operands),
        name="stats_out_kernel",
    )(*operands, held)
    cotangent = in_vmem(
        cotangent_kernel,
        rows_bf16,
        output,
        output_tangent,
        gain_out,
        curvature,
        *peers(stats),
    )
    all_cotangent, _ = gather_rows(cotangent)

    merged = 2 if len(starts) > 2 else 1
    slopes = [jnp.concatenate(slopes[:merged], axis=1)] + slopes[merged:]
    sizes = [sum(sizes[:merged])] + sizes[merged:]
    starts = [0] + starts[merged:]
    totals, lhs = [], all_cotangent
    for start, chunk in zip(starts, sizes):
        own, other = back_parts(lhs, held, start, chunk, *totals[:-1])
        totals.append(own + swap_tensor(other, 1).astype(F32))
        lhs = after(all_cotangent, own)
    down_product = outer_rows(hiddens, all_cotangent, down_weight.shape, *totals)

    made = [down_product]
    for j, (start, chunk) in enumerate(zip(starts, sizes)):
        total = over_tensor(totals[j], made[max(0, j - 1)])
        grad = (total * slopes[j].astype(F32)).astype(BF16)
        grad = jnp.concatenate([grad, swap_tensor(grad, 1)], axis=0)
        so_far = made[-1] if j else None
        made.append(outer_columns(all_normed, grad, up_weight.shape, start, so_far))
    up_product = made[-1]
    return (up_product, down_product)


def solution(mesh):
    return jax.shard_map(
        on_device,
        mesh=mesh,
        in_specs=(
            P("dp", "tensor"),
            P("tensor"),
            P("tensor"),
            P("tensor", "dp"),
            P("dp"),
            P("dp", "tensor"),
            P("tensor"),
            P("dp", "tensor"),
            P("tensor", "dp"),
            P("dp", "tensor"),
        ),
        out_specs=(P("tensor", "dp"), P("dp", "tensor")),
        check_vma=False,
    )
```

```python
import functools

import jax
import jax.numpy as jnp
from jax import lax
from jax.experimental import pallas as pl
from jax.experimental.pallas import tpu as pltpu
from jax.sharding import PartitionSpec as P

D = 6144
TILE = 256
LANES = 128
LOADS = 4
SLOTS = 6
SCALE = 1000
BF16 = jnp.bfloat16
F32 = jnp.float32
PARAMS = pltpu.CompilerParams(vmem_limit_bytes=20 * 1024 * 1024)


epsilon = 1e-05
root_half = 0.7071067811865476
inv_root_two_pi = 0.3989422804014327


def swap_tensor(value, flip):
    size = lax.axis_size("tensor")
    return lax.ppermute(value, "tensor", [(t, t ^ flip) for t in range(size)])


def swap_dp(value, flip):
    size = lax.axis_size("dp")
    return lax.ppermute(value, "dp", [(i, i ^ flip) for i in range(size)])


def after(value, *earlier):
    return lax.optimization_barrier((value, *earlier))[0]


def swap_rows(values):
    half = values.shape[0] // 2
    return jnp.concatenate([values[half:], values[:half]], axis=0)


def far_bits():
    return [1 << k for k in range(1, lax.axis_size("dp").bit_length() - 1)]


def gather_rows(value, beside=None):
    half = value.shape[0] // 2
    count = lax.axis_size("dp")
    held = {0: value}
    for bit in reversed(far_bits()):
        held |= {far | bit: swap_dp(block, bit) for far, block in held.items()}
    held |= {far | 1: swap_dp(block, 1) for far, block in held.items()}
    made = beside(held[count - 2]) if beside else ()
    blocks = [held[place] for place in range(count - 1)] + [after(held[count - 1], *made)]
    rows = jnp.concatenate(
        [block[:half] for block in blocks] + [block[half:] for block in blocks], axis=0
    )
    return rows, made


def scatter_rows(parts, rows):
    half = rows // 2
    count = lax.axis_size("dp")

    def block(place):
        cuts = [
            part[k * count * half + place * half : k * count * half + (place + 1) * half]
            for part in parts
            for k in (0, 1)
        ]
        return jnp.concatenate(cuts, axis=0)

    order = list(range(count - 2, -1, -2))
    terms = {}
    for k, far in enumerate(order):
        sent = block(far + 1).astype(BF16)
        if k >= 2:
            sent = after(sent, *[terms[o][1] for o in order[: k - 1]])
        terms[far] = [block(far), swap_dp(sent, 1)]
    pending = [(far, bit) for bit in far_bits() for far in order if far & bit and far & (bit - 1) < 2]
    pending.sort(key=lambda step: [-step[0], step[1]])
    last = []
    for far, bit in pending:
        total = sum(term.astype(F32) for term in terms[far]).astype(BF16)
        total = after(total, *last) if last else total
        last = [total]
        terms[far ^ bit].append(swap_dp(total, bit))
    return terms[0], last[0]


def cost(flops, *arrays):
    moved = sum(a.size * a.dtype.itemsize for a in arrays)
    return pl.CostEstimate(
        flops=int(flops) // SCALE, bytes_accessed=int(moved) // SCALE, transcendentals=0
    )


def load_kernel(start, count, *refs):
    refs, sems = refs[:count] + refs[-1 - count : -1], refs[-1]
    copies = []
    for k in range(count):
        given, held = refs[k], refs[count + k]
        rows, width = held.shape
        step = rows // LOADS
        for n in range(LOADS):
            cut = pl.ds(n * step, step)
            place = given.at[cut, pl.ds(start, width)]
            copies.append(pltpu.make_async_copy(place, held.at[cut], sems.at[k * LOADS + n]))
            copies[-1].start()
    for copy in copies:
        copy.wait()


def load_columns(arrays, start, width, *earlier):
    rows = arrays[0].shape[0]
    parts = [jax.ShapeDtypeStruct((rows, width), a.dtype) for a in arrays]
    return pl.pallas_call(
        functools.partial(load_kernel, start, len(arrays)),
        in_specs=[pl.BlockSpec(memory_space=pl.ANY)] * (len(arrays) + len(earlier)),
        out_specs=[pl.BlockSpec(memory_space=pltpu.VMEM)] * len(arrays),
        out_shape=[pltpu.VMEM(p.shape, p.dtype) for p in parts],
        scratch_shapes=[pltpu.SemaphoreType.DMA((LOADS * len(arrays),))],
        compiler_params=PARAMS,
        cost_estimate=cost(0, *parts),
        name="load_columns",
    )(*[pltpu.with_memory_space_constraint(a, pltpu.HBM) for a in arrays], *earlier)


def load_rows(array, start, height, *earlier):
    def kernel(given_ref, *refs):
        held, sems = refs[-2:]
        step = height // LOADS
        copies = []
        for n in range(LOADS):
            place = given_ref.at[pl.ds(start + n * step, step)]
            copies.append(pltpu.make_async_copy(place, held.at[pl.ds(n * step, step)], sems.at[n]))
            copies[n].start()
        for copy in copies:
            copy.wait()

    return pl.pallas_call(
        kernel,
        in_specs=[pl.BlockSpec(memory_space=pl.ANY)] * (1 + len(earlier)),
        out_specs=pl.BlockSpec(memory_space=pltpu.VMEM),
        out_shape=pltpu.VMEM((height, array.shape[1]), array.dtype),
        scratch_shapes=[pltpu.SemaphoreType.DMA((LOADS,))],
        compiler_params=PARAMS,
        cost_estimate=cost(0, array),
        name="load_rows",
    )(pltpu.with_memory_space_constraint(array, pltpu.HBM), *earlier)


def back_kernel(first, rows_ref, weight_ref, *refs):
    own_ref, other_ref = refs[-2:]
    half, chunk = own_ref.shape
    for start in range(0, chunk, TILE):
        part = lax.dot_general(
            rows_ref[...],
            weight_ref[first + start : first + start + TILE],
            (((1,), (1,)), ((), ())),
            preferred_element_type=F32,
        )
        own_ref[:, start : start + TILE] = part[:half]
        other_ref[:, start : start + TILE] = part[half:].astype(BF16)


def back_parts(cotangent, weight, start, chunk, *earlier):
    rows, width = cotangent.shape
    half = rows // 2
    vmem, anywhere = pl.BlockSpec(memory_space=pltpu.VMEM), pl.BlockSpec(memory_space=pl.ANY)
    return pl.pallas_call(
        functools.partial(back_kernel, start),
        in_specs=[vmem, vmem] + [anywhere] * len(earlier),
        out_shape=(
            jax.ShapeDtypeStruct((half, chunk), F32),
            jax.ShapeDtypeStruct((half, chunk), BF16),
        ),
        compiler_params=PARAMS,
        cost_estimate=cost(2 * rows * width * chunk, cotangent),
        name="back_parts",
    )(cotangent, pltpu.with_memory_space_constraint(weight, pltpu.VMEM), *earlier)


def up_kernel(rows_ref, weight_ref, tangent_ref, own_ref, other_ref):
    half = own_ref.shape[1]
    for start in range(0, own_ref.shape[2], TILE):
        cut = slice(start, start + TILE)
        for k, ref in enumerate((weight_ref, tangent_ref)):
            part = jnp.dot(rows_ref[...], ref[:, cut], preferred_element_type=F32)
            own_ref[k, :, cut] = part[:half]
            other_ref[k, :, cut] = part[half:].astype(BF16)


def up_parts(normed, weight, tangent):
    rows, width = normed.shape
    half, chunk = rows // 2, weight.shape[1]
    out_shape = (
        jax.ShapeDtypeStruct((2, half, chunk), F32),
        jax.ShapeDtypeStruct((2, half, chunk), BF16),
    )
    held = [pltpu.with_memory_space_constraint(a, pltpu.VMEM) for a in (weight, tangent)]
    return pl.pallas_call(
        up_kernel,
        out_shape=out_shape,
        compiler_params=PARAMS,
        cost_estimate=cost(4 * rows * width * chunk, normed),
        name="up_parts",
    )(normed, *held)


def outer(left, right):
    return lax.dot_general(left, right, (((0,), (0,)), ((), ())), preferred_element_type=F32)


def columns_kernel(column, left_ref, right_ref, *refs):
    out_ref, held, sems = refs[-3:]
    width = right_ref.shape[1]
    copies = []
    for k in range(held.shape[0]):
        held[k] = outer(left_ref[:, k * TILE : (k + 1) * TILE], right_ref[...])
        place = out_ref.at[pl.ds(k * TILE, TILE), pl.ds(column, width)]
        copies.append(pltpu.make_async_copy(held.at[k], place, sems.at[k]))
        copies[-1].start()
    for copy in copies:
        copy.wait()


def outer_columns(left, right, shape, column, so_far):
    tiles = left.shape[1] // TILE
    moved = jax.ShapeDtypeStruct((left.shape[1], right.shape[1]), F32)
    vmem, anywhere = pl.BlockSpec(memory_space=pltpu.VMEM), pl.BlockSpec(memory_space=pl.ANY)
    more = [] if so_far is None else [so_far]
    return pl.pallas_call(
        functools.partial(columns_kernel, column),
        in_specs=[vmem, vmem] + [anywhere] * len(more),
        out_specs=anywhere,
        out_shape=jax.ShapeDtypeStruct(shape, F32),
        scratch_shapes=[
            pltpu.VMEM((tiles, TILE, right.shape[1]), F32),
            pltpu.SemaphoreType.DMA((tiles,)),
        ],
        input_output_aliases={2: 0} if more else {},
        compiler_params=PARAMS,
        cost_estimate=cost(2 * left.size * right.shape[1], left, right, moved),
        name="outer_columns",
    )(left, right, *more)


def rows_kernel(count, *refs):
    left_refs, right_ref = refs[:count], refs[count]
    out_ref, held, sems = refs[-3:]
    slots = held.shape[0]
    copies = []
    for left_ref in left_refs:
        for start in range(0, left_ref.shape[1], TILE):
            k = len(copies)
            slot = k % slots
            if k >= slots:
                copies[k - slots].wait()
            held[slot] = outer(left_ref[:, start : start + TILE], right_ref[...])
            place = out_ref.at[pl.ds(k * TILE, TILE)]
            copies.append(pltpu.make_async_copy(held.at[slot], place, sems.at[slot]))
            copies[k].start()
    for copy in copies[-slots:]:
        copy.wait()


def outer_rows(lefts, right, shape, *earlier):
    slots = min(SLOTS, shape[0] // TILE)
    vmem = pl.BlockSpec(memory_space=pltpu.VMEM)
    moved = jax.ShapeDtypeStruct(shape, F32)
    return pl.pallas_call(
        functools.partial(rows_kernel, len(lefts)),
        in_specs=[vmem] * (len(lefts) + 1) + [pl.BlockSpec(memory_space=pl.ANY)] * len(earlier),
        out_specs=pl.BlockSpec(memory_space=pl.ANY),
        out_shape=moved,
        scratch_shapes=[
            pltpu.VMEM((slots, TILE, shape[1]), F32),
            pltpu.SemaphoreType.DMA((slots,)),
        ],
        compiler_params=PARAMS,
        cost_estimate=cost(2 * right.size * shape[0], right, moved),
        name="outer_rows",
    )(*lefts, right, *earlier)


def row_sum(values):
    return jnp.sum(values, axis=1, keepdims=True)


def put_columns(ref, values):
    lane = lax.broadcasted_iota(jnp.int32, ref.shape, 1)
    total = jnp.zeros(ref.shape, F32)
    for k, value in enumerate(values):
        total = jnp.where(lane == k, value, total)
    ref[...] = total


def get_columns(refs, count):
    found = []
    for flip, ref in enumerate(refs):
        values = ref[...]
        if flip & 1:
            values = swap_rows(values)
        found.append([values[:, k : k + 1] for k in range(count)])
    return found


def swap_if(flag, values):
    return jnp.where(flag == 1, swap_rows(values), values)


def stats_in_kernel(odd_ref, given_ref, tokens_ref, stats_ref):
    tokens_ref[...] = swap_if(odd_ref[0], given_ref[...])
    source = tokens_ref[...].astype(F32)
    mean = row_sum(source) / source.shape[1]
    put_columns(stats_ref, [mean, row_sum(jnp.square(source - mean))])


def norm_in_kernel(tokens_ref, gain_ref, shift_ref, *refs):
    source = tokens_ref[...].astype(F32)
    width = source.shape[1]
    stats = get_columns(refs[:-1], 2)
    center = sum(s[0] for s in stats) / len(stats)
    spread = sum(s[1] + width * jnp.square(s[0] - center) for s in stats) / D
    inverse = lax.rsqrt(spread + epsilon)
    refs[-1][...] = ((source - center) * inverse * gain_ref[...] + shift_ref[...]).astype(BF16)


def stats_out_kernel(count, tokens_ref, gain_ref, curvature_ref, *refs):
    terms = refs[:count]
    output_ref, tangent_ref, stats_ref = refs[-3:]
    rows, width = output_ref.shape
    total = sum(term[...].astype(F32) for term in terms)
    output = tokens_ref[...].astype(F32) + total[:rows]
    tangent = total[rows:]
    output_ref[...] = output
    tangent_ref[...] = tangent
    factor = gain_ref[...] * gain_ref[...] * curvature_ref[...]
    output_mean, tangent_mean = row_sum(output) / width, row_sum(tangent) / width
    output_off, tangent_off = output - output_mean, tangent - tangent_mean
    factor_output = factor * output_off
    put_columns(
        stats_ref,
        [
            output_mean,
            tangent_mean,
            row_sum(output_off * output_off),
            row_sum(output_off * tangent_off),
            row_sum(factor),
            row_sum(factor_output),
            row_sum(factor * tangent_off),
            row_sum(factor_output * output_off),
            row_sum(factor_output * tangent_off),
        ],
    )


def cotangent_kernel(output_ref, tangent_ref, gain_ref, curvature_ref, *refs):
    output, tangent = output_ref[...], tangent_ref[...]
    width = output.shape[1]
    stats = get_columns(refs[:-1], 9)
    center = sum(s[0] for s in stats) / len(stats)
    center_tangent = sum(s[1] for s in stats) / len(stats)
    square = cross = f_output = f_tangent = f_square = f_cross = 0.0
    for mean_o, mean_t, oo, ot, f, fo, ft, foo, fot in stats:
        a, b = mean_o - center, mean_t - center_tangent
        square += oo + width * a * a
        cross += ot + width * a * b
        f_output += fo + a * f
        f_tangent += ft + b * f
        f_square += foo + a * (2.0 * fo + a * f)
        f_cross += fot + a * ft + b * (fo + a * f)
    inverse = lax.rsqrt(square / D + epsilon)
    tangent_dot = cross * inverse / D
    weight_mean = (f_tangent - tangent_dot * inverse * f_output) * inverse / D
    weight_dot = (f_cross - tangent_dot * inverse * f_square) * inverse * inverse / D
    normal = (output - center) * inverse
    factor = gain_ref[...] * gain_ref[...] * curvature_ref[...]
    weighted = factor * ((tangent - center_tangent - normal * tangent_dot) * inverse)
    refs[-1][...] = ((weighted - weight_mean - normal * weight_dot) * inverse).astype(BF16)


def in_vmem(kernel, out_shape, *operands):
    return pl.pallas_call(
        kernel,
        out_shape=out_shape,
        compiler_params=PARAMS,
        cost_estimate=cost(0, *operands),
        name=kernel.__name__,
    )(*operands)


def peers(value):
    return [value] + [swap_tensor(value, flip) for flip in range(1, lax.axis_size("tensor"))]


def over_tensor(total, *earlier):
    flip = 2
    while flip < lax.axis_size("tensor"):
        received = swap_tensor(total.astype(BF16), flip)
        if earlier:
            received = after(received, *earlier)
        total = total + received.astype(F32)
        flip *= 2
    return total


def chunks_of(units):
    part = units // 12
    sizes = [2 * part, 3 * part, 4 * part, 3 * part] if part % TILE == 0 else [units]
    return [sum(sizes[:k]) for k in range(len(sizes))], sizes


def on_device(
    tokens,
    gain_in,
    shift_in,
    up_weight,
    up_bias,
    down_weight,
    gain_out,
    curvature,
    up_tangent,
    down_tangent,
):
    rows, width = tokens.shape
    hidden_units = up_weight.shape[1]
    starts, sizes = chunks_of(hidden_units)
    odd = lax.axis_index("tensor") & 1
    curvature = swap_if(odd, curvature)
    gain_in, shift_in, gain_out = gain_in[None], shift_in[None], gain_out[None]
    stats_shape = jax.ShapeDtypeStruct((rows, LANES), F32)
    rows_bf16 = jax.ShapeDtypeStruct((rows, width), BF16)
    rows_f32 = jax.ShapeDtypeStruct((rows, width), F32)

    tokens, stats = pl.pallas_call(
        stats_in_kernel,
        in_specs=[
            pl.BlockSpec(memory_space=pltpu.SMEM),
            pl.BlockSpec(memory_space=pltpu.VMEM),
        ],
        out_shape=(rows_bf16, stats_shape),
        compiler_params=PARAMS,
        cost_estimate=cost(0, tokens),
        name="stats_in_kernel",
    )(odd.astype(jnp.int32)[None], tokens)
    stats = peers(stats)
    normed = in_vmem(norm_in_kernel, rows_bf16, tokens, gain_in, shift_in, *stats)
    all_normed, weights = gather_rows(
        normed,
        lambda early: load_columns((after(up_weight, early), up_tangent), starts[0], sizes[0]),
    )

    totals, owns, own = [], [], None
    for j, (start, chunk) in enumerate(zip(starts, sizes)):
        if j:
            weights = load_columns((after(up_weight, own), up_tangent), start, chunk, totals[-1])
        lhs = after(all_normed, totals[-1], *weights) if j else all_normed
        own, other = up_parts(lhs, *weights)
        totals.append(own + swap_tensor(other, 1).astype(F32))
        owns.append(own)

    slopes, hiddens, done = [], [], [()]
    primal = tangent = None
    for j, (start, chunk) in enumerate(zip(starts, sizes)):
        total = over_tensor(totals[j], *([both if j == len(starts) - 1 else mine, *done[j - 1]] if j else owns[1:2]))
        if j:
            total = after(total, totals[min(j + 2, len(totals) - 1)])
        pre = total[0] + up_bias[start : start + chunk]
        cumulative = 0.5 * (1.0 + lax.erf(pre * root_half))
        slope = cumulative + pre * jnp.exp(-0.5 * pre * pre) * inv_root_two_pi
        slopes.append(slope.astype(BF16))
        mine = jnp.stack([(pre * cumulative).astype(BF16), (slope * total[1]).astype(BF16)])
        both = jnp.concatenate([mine, swap_tensor(mine, 1)], axis=1)
        hidden, hidden_tangent = both[0], both[1]
        hiddens.append(hidden)
        weight = down_weight[start : start + chunk]
        primal_part = jnp.dot(hidden, weight, preferred_element_type=F32)
        tangent_part = jnp.dot(hidden_tangent, weight, preferred_element_type=F32) + jnp.dot(
            hidden, down_tangent[start : start + chunk], preferred_element_type=F32
        )
        primal = primal_part if primal is None else primal + primal_part
        tangent = tangent_part if tangent is None else tangent + tangent_part
        done.append((primal, tangent))

    terms, step = scatter_rows([primal, tangent], rows)
    held = load_rows(down_weight, 0, hidden_units, step)
    operands = [tokens, gain_out, curvature, *terms]
    vmem = pl.BlockSpec(memory_space=pltpu.VMEM)
    output, output_tangent, stats = pl.pallas_call(
        functools.partial(stats_out_kernel, len(terms)),
        in_specs=[vmem] * len(operands) + [pl.BlockSpec(memory_space=pl.ANY)],
        out_shape=(rows_f32, rows_f32, stats_shape),
        compiler_params=PARAMS,
        cost_estimate=cost(0, *operands),
        name="stats_out_kernel",
    )(*operands, held)
    cotangent = in_vmem(
        cotangent_kernel,
        rows_bf16,
        output,
        output_tangent,
        gain_out,
        curvature,
        *peers(stats),
    )
    all_cotangent, _ = gather_rows(cotangent)

    merged = 2 if len(starts) > 2 else 1
    slopes = [jnp.concatenate(slopes[:merged], axis=1)] + slopes[merged:]
    sizes = [sum(sizes[:merged])] + sizes[merged:]
    starts = [0] + starts[merged:]
    totals, lhs = [], all_cotangent
    for start, chunk in zip(starts, sizes):
        own, other = back_parts(lhs, held, start, chunk, *totals[:-1])
        totals.append(own + swap_tensor(other, 1).astype(F32))
        lhs = after(all_cotangent, own)
    down_product = outer_rows(hiddens, all_cotangent, down_weight.shape, *totals)

    made = [down_product]
    for j, (start, chunk) in enumerate(zip(starts, sizes)):
        total = over_tensor(totals[j], made[max(0, j - 1)])
        grad = (total * slopes[j].astype(F32)).astype(BF16)
        grad = jnp.concatenate([grad, swap_tensor(grad, 1)], axis=0)
        so_far = made[-1] if j else None
        made.append(outer_columns(all_normed, grad, up_weight.shape, start, so_far))
    up_product = made[-1]
    return (up_product, down_product)


def solution(mesh):
    return jax.shard_map(
        on_device,
        mesh=mesh,
        in_specs=(
            P("dp", "tensor"),
            P("tensor"),
            P("tensor"),
            P("tensor", "dp"),
            P("dp"),
            P("dp", "tensor"),
            P("tensor"),
            P("dp", "tensor"),
            P("tensor", "dp"),
            P("dp", "tensor"),
        ),
        out_specs=(P("tensor", "dp"), P("dp", "tensor")),
        check_vma=False,
    )
```
